32 devices in a mesh: chan: 4 (over y, x), tile: 8 (over z, core).
Axes of the slice: x: 2, y: 2, z: 4, core: 2. Of those that a mesh axis runs over, the one named last changes fastest.
Arguments:
- visibilities: bfloat16 [8192, 1024], P('tile', 'chan'), parts along dimension 1, may hold values from -6 to 6
- send_list: int32 [256, 128], P(('chan', 'tile')), parts along dimension 0, may hold values from -1 to 1023, as said below
- pixels: int32 [2, 32768], P(None, ('chan', 'tile')), parts along dimension 1, may hold values from 0 to 31
- offsets: int32 [2, 32768], P(None, ('chan', 'tile')), parts along dimension 1, may hold values from 0 to 15
- taper: float32 [8, 16], replicated, may hold values from 0.1 to 0.6
Outputs:
- tiles: float32 [8, 32, 32, 1024], P('tile', None, None, 'chan'), parts along dimension 3
The draws below stay inside these ranges and needn't reach their ends.
There are 4 independent parts, one for each index of `chan`. The reference program is written for one: setup_inputs(seed, part) draws one part's arguments, and reference() takes and returns one part's arrays. A program takes and returns all parts, laid end to end along the dimension named above; an argument that names none is the same for every part. Nothing has to cross between parts.
Inputs may be any that keep to these rules, and one draw needn't show every extreme that they name: `send_list`: for every sender and tile the live entries come first and are distinct local row indices; no row is listed twice by one sender; the rest are -1. One tile, drawn from the seed, gets 128 live slots from every sender, and every sender lists its last row.
All inputs are finite; a program needn't handle non-finite values.
Results may differ from the reference program's by a relative error of at most 0.0029.
Values may be sent and summed in bfloat16 or wider, within the bound.
A program may use at most 64 MiB of HBM per device.

```python
import jax
import jax.numpy as jnp
from jax import lax

CH = 128
TS = 32
ROWS_DEV = 1024
TAPS = 8
OS = 16
TILES_Y = 8
TILES_X = 1
CAP = 128
ROWS_ALL = 8192
N_TILE = 8


def draw_send_list(key, part):
    center_key = jax.random.fold_in(key, 7001)
    center_x = jax.random.randint(jax.random.fold_in(center_key, 1), (), 0, N_TILE // TILES_Y)
    center_y = jax.random.randint(jax.random.fold_in(center_key, 2), (), 0, TILES_Y)
    tile_ids = jnp.arange(N_TILE, dtype=jnp.int32)
    distance = (tile_ids // TILES_Y - center_x) ** 2 + (tile_ids % TILES_Y - center_y) ** 2
    reach = 2 * N_TILE
    slot_ids = jnp.arange(CAP, dtype=jnp.int32)

    def one_sender(sender):
        sender_key = jax.random.fold_in(key, sender + 100)
        jitter = jax.random.randint(jax.random.fold_in(sender_key, 1), (N_TILE,), 0, CAP // 2 + 1)
        jitter = jnp.where(distance > 0, jitter, 0)
        counts = jnp.clip(CAP - distance * CAP // reach - jitter, 0, CAP)
        ordering = jax.random.permutation(jax.random.fold_in(sender_key, 2), ROWS_DEV).astype(jnp.int32)
        leading = ordering[0]
        ordering = jnp.where(ordering == ROWS_DEV - 1, leading, ordering).at[0].set(ROWS_DEV - 1)
        starts = jnp.cumsum(counts) - counts
        chosen = ordering[jnp.clip(starts[:, None] + slot_ids[None, :], 0, ROWS_DEV - 1)]
        return jnp.where(slot_ids[None, :] < counts[:, None], chosen, -1)
    listed = jax.vmap(one_sender)(jnp.arange(N_TILE, dtype=jnp.int32))
    return listed.reshape(N_TILE * N_TILE, CAP).astype(jnp.int32)


def set_ends(array, stream_key, low, high):
    dims = array.shape
    spot = [jax.random.randint(jax.random.fold_in(stream_key, axis), (), 0, dims[axis]) for axis in range(len(dims))]
    array = array.at[tuple(spot)].set(low)
    longest = dims.index(max(dims))
    spot[longest] = (spot[longest] + 1) % dims[longest]
    return array.at[tuple(spot)].set(high)


def block_scale(key, dims, split, low, largest):
    def one(position, shards_of):
        draws = jax.random.uniform(jax.random.fold_in(jax.random.fold_in(key, 6), position), (shards_of,), jnp.float32, low / len(split), largest / len(split))
        return jnp.repeat(jnp.exp(draws), dims[position] // shards_of).reshape((-1,) + (1,) * (len(dims) - position - 1))

    gain = one(*split[0])
    for cut in split[1:]:
        gain = gain * one(*cut)
    return gain


def normal_values(stream_key, extent, spread, most, pieces=(), held_as=jnp.bfloat16):
    gain = block_scale(stream_key, extent, pieces, -0.22, 0.18) if pieces else 1.0
    values = jax.random.normal(stream_key, extent, jnp.float32) * spread * gain
    return jnp.minimum(jnp.maximum(values, -most), most).astype(held_as)


def setup_inputs(seed: int = 0, part: int = 0) -> dict:
    key_list = jax.random.split(jax.random.key(seed), 6)
    own_keys = jax.random.split(jax.random.fold_in(key_list[5], part), 6)
    return {
        "visibilities": normal_values(own_keys[0], (ROWS_ALL, 2 * CH), 1.0, 6.0, ((0, 8),)),
        "send_list": draw_send_list(jax.random.fold_in(jax.random.fold_in(key_list[5], part), 71), part),
        "pixels": set_ends(jax.random.randint(own_keys[2], (2, ROWS_ALL), 0, TS), jax.random.fold_in(own_keys[2], 1), 0, TS - 1).astype(jnp.int32),
        "offsets": set_ends(jax.random.randint(own_keys[3], (2, ROWS_ALL), 0, OS), jax.random.fold_in(own_keys[3], 1), 0, OS - 1).astype(jnp.int32),
        "taper": jnp.clip(jax.random.uniform(key_list[4], (TAPS, OS), jnp.float32, 0.1, 0.6), 0.1, 0.6),
    }


def reference(visibilities, send_list, pixels, offsets, taper):
    components = visibilities.shape[1]
    width_x = TILES_X * TS + 8
    width_y = TILES_Y * TS + 8
    slot_total = N_TILE * CAP
    destination = jnp.arange(slot_total, dtype=jnp.int32) // CAP
    base_x = (destination // TILES_Y) * TS
    base_y = (destination % TILES_Y) * TS
    tap_index = jnp.arange(TAPS, dtype=jnp.int32)

    def per_sender(canvas, sender):
        listed = lax.dynamic_slice_in_dim(send_list, (sender * N_TILE).astype(jnp.int32), N_TILE, 0).reshape(-1)
        is_live = listed >= 0
        picked = (jnp.where(is_live, listed, 0) + sender * ROWS_DEV).astype(jnp.int32)
        slot_rows = jnp.take(visibilities, picked, axis=0).astype(jnp.float32) * is_live[:, None].astype(jnp.float32)
        kernel_u = jnp.take(taper, jnp.take(offsets[0], picked), axis=1)
        kernel_v = jnp.take(taper, jnp.take(offsets[1], picked), axis=1)
        weights = lax.optimization_barrier((kernel_u[:, None, :] * kernel_v[None, :, :]).astype(jnp.bfloat16))
        weights = weights.astype(jnp.float32)
        pos_x = base_x + jnp.take(pixels[0], picked)
        pos_y = base_y + jnp.take(pixels[1], picked)
        for tap_u in range(TAPS):
            flat_index = ((pos_x + tap_u)[None, :] * width_y + pos_y[None, :] + tap_index[:, None]).reshape(-1)
            values = (weights[tap_u][:, :, None] * slot_rows[None, :, :]).reshape(-1, components)
            canvas = canvas.at[flat_index].add(values)
        return canvas, None

    canvas = jnp.zeros((width_x * width_y, components), jnp.float32)
    canvas, _ = lax.scan(per_sender, canvas, jnp.arange(N_TILE, dtype=jnp.int32))
    grid = canvas.reshape(width_x, width_y, components)[4:width_x - 4, 4:width_y - 4]
    grid = grid.reshape(TILES_X, TS, TILES_Y, TS, components).transpose(0, 2, 1, 3, 4)
    return grid.reshape(N_TILE, TS, TS, components)
```

```python
import jax
import jax.numpy as jnp
from jax import lax
from jax.experimental import pallas as pl
from jax.experimental.pallas import tpu as pltpu
from jax.sharding import PartitionSpec as P

TS = 32
TILES_Y = 8
RIM = 4
LANES = 128
MESH = pl.DeviceIdType.MESH


def flip(index, distance):
    total = 0
    for bit in (1, 2, 4):
        own = (index // bit) % 2
        total = total + bit * (1 - own if distance & bit else own)
    return total


def line_kernel(
    vis, lists, pix, off, taper, out,
    rows_out, rows_in, meta_out, meta_in, w_main, w_rim, rim_sum, rim_out, rim_in,
    row_send, row_recv, meta_send, meta_recv, rim_send, rim_recv,
):
    count, slots = lists.shape
    rows, width = vis.shape
    taps, levels = taper.shape
    me = lax.axis_index("tile")
    far_first = [d for d in range(count - 1, 1, -1)] + [1]
    peers = {d: flip(me, d) for d in range(1, count)}

    barrier = pltpu.get_barrier_semaphore()
    for d in far_first:
        pl.semaphore_signal(barrier, inc=1, device_id={"tile": peers[d]}, device_id_type=MESH)

    listed = lists[...]
    live = listed >= 0
    spot = jnp.where(live, listed, 0)
    packed = pix[0:1, :] + 32 * pix[1:2, :] + 1024 * off[0:1, :] + 16384 * off[1:2, :]
    inner = spot & (LANES - 1)
    outer = spot >> 7
    found = jnp.zeros((count, slots), jnp.int32)
    for b in range(rows // LANES):
        source = jnp.broadcast_to(packed[:, b * LANES : (b + 1) * LANES], (count, LANES))
        here = jnp.take_along_axis(source, inner, axis=1, mode="promise_in_bounds")
        found = jnp.where(outer == b, here, found)
    fields = (
        jnp.where(live, found & 31, -64),
        jnp.where(live, (found >> 5) & 31, -64),
        (found >> 10) & 15,
        (found >> 14) & 15,
    )
    for t in range(count):
        for f, field in enumerate(fields):
            meta_out[t, f : f + 1, :] = field[t : t + 1, :]

    pl.semaphore_wait(barrier, count - 1)

    def meta_copy(d):
        return pltpu.make_async_remote_copy(
            src_ref=meta_out.at[peers[d]], dst_ref=meta_in.at[me],
            send_sem=meta_send.at[d], recv_sem=meta_recv.at[d],
            device_id={"tile": peers[d]}, device_id_type=MESH,
        )

    def row_copy(d):
        return pltpu.make_async_remote_copy(
            src_ref=rows_out.at[d], dst_ref=rows_in.at[me],
            send_sem=row_send.at[d], recv_sem=row_recv.at[d],
            device_id={"tile": peers[d]}, device_id_type=MESH,
        )

    for d in far_first:
        meta_copy(d).start()
    meta_in[me] = meta_out[me]

    lane = lax.broadcasted_iota(jnp.int32, (slots, LANES), 1)

    def pick(t):
        row = lists[pl.ds(t, 1), :]
        spread_list = jnp.broadcast_to(row, (LANES, slots)).T
        hot = [
            jnp.where(spread_list == lane + b * LANES, 1.0, 0.0).astype(jnp.bfloat16)
            for b in range(rows // LANES)
        ]
        return jnp.concatenate(hot, axis=1)

    for d in range(count - 2, -1, -2):
        near = me if d == 0 else peers[d]
        hot = jnp.concatenate([pick(near), pick(peers[d + 1])], axis=0)
        got = jnp.dot(hot, vis[...], preferred_element_type=jnp.float32).astype(jnp.bfloat16)
        if d == 0:
            rows_in[me] = got[:slots]
        else:
            rows_out[d] = got[:slots]
            row_copy(d).start()
        rows_out[d + 1] = got[slots:]
        row_copy(d + 1).start()

    for d in far_first:
        meta_copy(d).wait_recv()

    cell = lax.broadcasted_iota(jnp.int32, (TS, slots), 0) + RIM
    edge = lax.broadcasted_iota(jnp.int32, (2 * RIM, slots), 0)
    edge = jnp.where(edge >= RIM, edge + TS, edge)

    def spread(kernel, pixel, cells):
        tap = cells - pixel
        total = jnp.zeros(cells.shape, jnp.float32)
        for a in range(taps):
            total = jnp.where(tap == a, kernel[a : a + 1, :], total)
        return total

    def build(s, carry):
        meta = meta_in[s]
        kernel_u = jnp.zeros((taps, slots), jnp.float32)
        kernel_v = jnp.zeros((taps, slots), jnp.float32)
        for o in range(levels):
            column = jnp.broadcast_to(taper[:, o : o + 1], (taps, slots))
            kernel_u = jnp.where(meta[2:3, :] == o, column, kernel_u)
            kernel_v = jnp.where(meta[3:4, :] == o, column, kernel_v)
        spread_u = spread(kernel_u, meta[0:1, :], cell)
        spread_v = spread(kernel_v, meta[1:2, :], cell)
        edge_v = spread(kernel_v, meta[1:2, :], edge)
        at = pl.ds(pl.multiple_of(s * slots, LANES), slots)
        for i in range(TS):
            w_main[i * TS : (i + 1) * TS, at] = (spread_u[i : i + 1, :] * spread_v).astype(
                jnp.bfloat16
            )
        for j in range(2 * RIM):
            w_rim[j * TS : (j + 1) * TS, at] = (spread_u * edge_v[j : j + 1, :]).astype(
                jnp.bfloat16
            )
        return carry

    lax.fori_loop(0, count, build, 0)

    for d in range(0, count, 2):
        if d:
            row_copy(d).wait_recv()
        row_copy(d + 1).wait_recv()
        pair = (me if d == 0 else peers[d]) // 2
        block = rows_in[pl.ds(2 * pair, 2)].reshape(2 * slots, width)
        at = pl.ds(pl.multiple_of(pair * 2 * slots, 2 * LANES), 2 * slots)
        term = jnp.dot(w_rim[:, at], block, preferred_element_type=jnp.float32)
        if d == 0:
            rim_sum[...] = term
        elif d < count - 2:
            rim_sum[...] += term
        else:
            whole = (rim_sum[...] + term).astype(jnp.bfloat16)
            rim_out[0] = whole[: RIM * TS]
            rim_out[1] = whole[RIM * TS :]

    has_low = me > 0
    has_high = me < count - 1

    def rim_copy(side):
        return pltpu.make_async_remote_copy(
            src_ref=rim_out.at[side], dst_ref=rim_in.at[1 - side],
            send_sem=rim_send.at[side], recv_sem=rim_recv.at[1 - side],
            device_id={"tile": me - 1 + 2 * side}, device_id_type=MESH,
        )

    def rim_arrival(side):
        return pltpu.make_async_remote_copy(
            src_ref=rim_out.at[side], dst_ref=rim_in.at[side],
            send_sem=rim_send.at[side], recv_sem=rim_recv.at[side],
            device_id={"tile": me - 1 + 2 * side}, device_id_type=MESH,
        )

    for side, present in ((0, has_low), (1, has_high)):
        @pl.when(present)
        def _(side=side):
            rim_copy(side).start()

    everything = rows_in[...].reshape(count * slots, width)
    part = TS * TS // 4
    for m in range(4):
        total = jnp.dot(
            w_main[m * part : (m + 1) * part, :], everything, preferred_element_type=jnp.float32
        )
        out[m * part // TS : (m + 1) * part // TS] = total.reshape(part // TS, TS, width)

    place = lax.broadcasted_iota(jnp.int32, (8 * TS, RIM * TS), 0)
    origin = lax.broadcasted_iota(jnp.int32, (8 * TS, RIM * TS), 1)
    for side, present in ((0, has_low), (1, has_high)):
        @pl.when(present)
        def _(side=side):
            rim_arrival(side).wait_recv()
            wanted = (origin % TS) * 8 + origin // TS + RIM * side
            put = jnp.where(place == wanted, 1.0, 0.0).astype(jnp.bfloat16)
            extra = jnp.dot(put, rim_in[side], preferred_element_type=jnp.float32)
            first = (TS - 8) * side
            out[:, first : first + 8, :] += extra.reshape(TS, 8, width)
            rim_copy(side).wait_send()

    for d in far_first:
        meta_copy(d).wait_send()
        row_copy(d).wait_send()


def line_body(visibilities, send_list, pixels, offsets, taper):
    count, slots = send_list.shape
    width = visibilities.shape[1]
    cells = TS * TS
    rim_cells = 2 * RIM * TS
    dma = pltpu.SemaphoreType.DMA
    vmem = pl.BlockSpec(memory_space=pltpu.VMEM)
    result = pl.pallas_call(
        line_kernel,
        out_shape=jax.ShapeDtypeStruct((TS, TS, width), jnp.float32),
        in_specs=[vmem] * 5,
        out_specs=vmem,
        scratch_shapes=[
            pltpu.VMEM((count, slots, width), jnp.bfloat16),
            pltpu.VMEM((count, slots, width), jnp.bfloat16),
            pltpu.VMEM((count, 8, slots), jnp.int32),
            pltpu.VMEM((count, 8, slots), jnp.int32),
            pltpu.VMEM((cells, count * slots), jnp.bfloat16),
            pltpu.VMEM((rim_cells, count * slots), jnp.bfloat16),
            pltpu.VMEM((rim_cells, width), jnp.float32),
            pltpu.VMEM((2, rim_cells // 2, width), jnp.bfloat16),
            pltpu.VMEM((2, rim_cells // 2, width), jnp.bfloat16),
            dma((count,)), dma((count,)), dma((count,)), dma((count,)), dma((2,)), dma((2,)),
        ],
        compiler_params=pltpu.CompilerParams(
            collective_id=0, has_side_effects=True, vmem_limit_bytes=48 * 1024 * 1024
        ),
    )(visibilities, send_list, pixels, offsets, taper)
    return result[None]


def passed_along(value, axis, by):
    count = lax.axis_size(axis)
    pairs = [(i, i + by) for i in range(count) if 0 <= i + by < count]
    return lax.ppermute(value, axis, pairs)


def spread(kernel, pixel, padded_side):
    cell_index = jnp.arange(padded_side, dtype=jnp.int32)[:, None] - pixel[None, :]
    tap_index = jnp.arange(kernel.shape[0], dtype=jnp.int32)[:, None, None]
    return jnp.sum(jnp.where(cell_index[None] == tap_index, kernel[:, None, :], 0.0), axis=0)


def place_block(block_rows, block_meta, taper, padded_side):
    levels = jnp.arange(taper.shape[1], dtype=jnp.int32)[:, None]
    select_u = (levels == block_meta[2][None, :]).astype(jnp.float32)
    select_v = (levels == block_meta[3][None, :]).astype(jnp.float32)
    kernel_u = jnp.dot(
        taper, select_u, precision=lax.Precision.HIGHEST, preferred_element_type=jnp.float32
    )
    kernel_v = jnp.dot(
        taper, select_v, precision=lax.Precision.HIGHEST, preferred_element_type=jnp.float32
    )
    spread_u = spread(kernel_u, block_meta[0], padded_side)
    spread_v = spread(kernel_v, block_meta[1], padded_side)
    weights = (spread_u[:, None, :] * spread_v[None, :, :]).astype(jnp.bfloat16)
    weights = weights.reshape(padded_side * padded_side, -1)
    return jnp.dot(weights, block_rows, preferred_element_type=jnp.float32)


def grid_blocks(slot_rows, slot_meta, taper, padded_side, block_size, block_count):
    width = slot_rows.shape[1]

    def one_block(index, running):
        start = index * block_size
        block_rows = lax.dynamic_slice_in_dim(slot_rows, start, block_size, 0)
        block_meta = lax.dynamic_slice_in_dim(slot_meta, start, block_size, 1)
        return running + place_block(block_rows, block_meta, taper, padded_side)

    initial = jnp.zeros((padded_side * padded_side, width), jnp.float32)
    return lax.fori_loop(0, block_count, one_block, initial)


def body(visibilities, send_list, pixels, offsets, taper):
    tile_count = lax.axis_size("tile")
    tiles_x = tile_count // TILES_Y
    slot_cap = send_list.shape[1]
    components = visibilities.shape[1]
    padded_side = TS + 8
    slot_total = tile_count * slot_cap
    block_size = min(512, slot_total)
    is_live = send_list >= 0
    picked = jnp.where(is_live, send_list, 0).reshape(-1)
    gathered = jnp.take(visibilities, picked, axis=0).reshape(tile_count, slot_cap, components)
    outgoing = jnp.where(is_live[:, :, None], gathered, jnp.zeros_like(gathered))
    live_flag = is_live.reshape(1, -1)
    slot_meta = jnp.concatenate(
        [
            jnp.take(pixels, picked, axis=1),
            jnp.take(offsets, picked, axis=1),
            live_flag.astype(jnp.int32),
        ],
        0,
    )
    slot_meta = (
        jnp.where(live_flag, slot_meta, 0).reshape(5, tile_count, slot_cap).transpose(1, 0, 2)
    )
    arrived_meta = lax.all_to_all(slot_meta, "tile", split_axis=0, concat_axis=0, tiled=True)
    meta_rows = arrived_meta.transpose(1, 0, 2).reshape(5, slot_total)
    arrived = lax.all_to_all(outgoing, "tile", split_axis=0, concat_axis=0, tiled=True)
    padded_grid = grid_blocks(
        arrived.reshape(slot_total, components),
        meta_rows,
        taper,
        padded_side,
        block_size,
        slot_total // block_size,
    )
    padded_grid = padded_grid.reshape(padded_side, padded_side, components)
    tile_row = lax.axis_index("tile") % TILES_Y
    source_start = {-1: TS + 4, 0: 4, 1: 0}
    target_start = {-1: 0, 0: 0, 1: TS - 4}
    span = {-1: 4, 0: TS, 1: 4}
    result = padded_grid[4 : TS + 4, 4 : TS + 4]
    for step_x in (-1, 0, 1):
        for step_y in (-1, 0, 1):
            if step_x == 0 and step_y == 0 or (step_x != 0 and tiles_x == 1):
                continue
            piece = padded_grid[
                source_start[step_x] : source_start[step_x] + span[step_x],
                source_start[step_y] : source_start[step_y] + span[step_y],
            ]
            incoming = passed_along(piece, "tile", -(step_x * TILES_Y + step_y))
            inside = (tile_row + step_y >= 0) & (tile_row + step_y < TILES_Y)
            incoming = jnp.where(inside, incoming, 0.0)
            result = result.at[
                target_start[step_x] : target_start[step_x] + span[step_x],
                target_start[step_y] : target_start[step_y] + span[step_y],
            ].add(incoming)
    return result[None]


def solution(mesh):
    placed = (
        P("tile", "chan"),
        P(("chan", "tile"), None),
        P(None, ("chan", "tile")),
        P(None, ("chan", "tile")),
        P(),
    )
    one_line = mesh.shape["tile"] == TILES_Y

    def chosen(visibilities, send_list, *rest):
        fits = one_line and send_list.shape[1] == LANES and visibilities.shape[0] % LANES == 0
        return (line_body if fits else body)(visibilities, send_list, *rest)

    return jax.shard_map(
        chosen, mesh=mesh, in_specs=placed, out_specs=P("tile", None, None, "chan"), check_vma=False
    )
```

```python
import jax
import jax.numpy as jnp
from jax import lax
from jax.experimental import pallas as pl
from jax.experimental.pallas import tpu as pltpu
from jax.sharding import PartitionSpec as P

TS = 32
TILES_Y = 8
RIM = 4
LANES = 128
MESH = pl.DeviceIdType.MESH


def flip(index, distance):
    total = 0
    for bit in (1, 2, 4):
        own = (index // bit) % 2
        total = total + bit * (1 - own if distance & bit else own)
    return total


def line_kernel(
    vis_far, lists_far, pix_far, off_far, taper_far, out,
    vis, lists, pix, off, taper, load_sem, rows_out, rows_in, meta_out, meta_in, w_main, w_rim, rim_sum, rim_out, rim_in,
    row_send, row_recv, meta_send, meta_recv, rim_send, rim_recv,
):
    count, slots = lists.shape
    rows, width = vis.shape
    taps, levels = taper.shape
    me = lax.axis_index("tile")
    far_first = [d for d in range(count - 1, 1, -1)] + [1]
    peers = {d: flip(me, d) for d in range(1, count)}

    barrier = pltpu.get_barrier_semaphore()
    for d in far_first:
        pl.semaphore_signal(barrier, inc=1, device_id={"tile": peers[d]}, device_id_type=MESH)
    loads = [
        pltpu.make_async_copy(far, near, load_sem.at[i])
        for i, (far, near) in enumerate(
            ((lists_far, lists), (pix_far, pix), (off_far, off), (taper_far, taper), (vis_far, vis))
        )
    ]
    for load in loads:
        load.start()

    for load in loads[:4]:
        load.wait()
    listed = lists[...]
    live = listed >= 0
    spot = jnp.where(live, listed, 0)
    packed = pix[0:1, :] + 32 * pix[1:2, :] + 1024 * off[0:1, :] + 16384 * off[1:2, :]
    inner = spot & (LANES - 1)
    outer = spot >> 7
    found = jnp.zeros((count, slots), jnp.int32)
    for b in range(rows // LANES):
        source = jnp.broadcast_to(packed[:, b * LANES : (b + 1) * LANES], (count, LANES))
        here = jnp.take_along_axis(source, inner, axis=1, mode="promise_in_bounds")
        found = jnp.where(outer == b, here, found)
    fields = (
        jnp.where(live, found & 31, -64),
        jnp.where(live, (found >> 5) & 31, -64),
        (found >> 10) & 15,
        (found >> 14) & 15,
    )
    for t in range(count):
        for f, field in enumerate(fields):
            meta_out[t, f : f + 1, :] = field[t : t + 1, :]

    def meta_copy(d):
        return pltpu.make_async_remote_copy(
            src_ref=meta_out.at[peers[d], 0:4], dst_ref=meta_in.at[me, 0:4],
            send_sem=meta_send.at[d], recv_sem=meta_recv.at[d],
            device_id={"tile": peers[d]}, device_id_type=MESH,
        )

    def row_copy(d):
        return pltpu.make_async_remote_copy(
            src_ref=rows_out.at[d], dst_ref=rows_in.at[me],
            send_sem=row_send.at[d], recv_sem=row_recv.at[d],
            device_id={"tile": peers[d]}, device_id_type=MESH,
        )

    lane = lax.broadcasted_iota(jnp.int32, (slots, LANES), 1)

    def pick(t):
        row = lists[pl.ds(t, 1), :]
        spread_list = jnp.broadcast_to(row, (LANES, slots)).T
        hot = [
            jnp.where(spread_list == lane + b * LANES, 1.0, 0.0).astype(jnp.bfloat16)
            for b in range(rows // LANES)
        ]
        return jnp.concatenate(hot, axis=1)

    loads[4].wait()
    for d in range(count - 2, -1, -2):
        near = me if d == 0 else peers[d]
        hot = jnp.concatenate([pick(near), pick(peers[d + 1])], axis=0)
        got = jnp.dot(hot, vis[...], preferred_element_type=jnp.float32).astype(jnp.bfloat16)
        rows_out[d + 1] = got[slots:]
        if d == 0:
            rows_in[me] = got[:slots]
        else:
            rows_out[d] = got[:slots]
        if d == count - 2:
            pl.semaphore_wait(barrier, count - 1)
            for e in far_first:
                meta_copy(e).start()
            meta_in[me] = meta_out[me]
        if d:
            row_copy(d).start()
        row_copy(d + 1).start()

    for d in far_first:
        meta_copy(d).wait_recv()

    cell = lax.broadcasted_iota(jnp.int32, (TS, slots), 0) + RIM
    edge = lax.broadcasted_iota(jnp.int32, (2 * RIM, slots), 0)
    edge = jnp.where(edge >= RIM, edge + TS, edge)

    def spread(kernel, pixel, cells):
        tap = cells - pixel
        total = jnp.zeros(cells.shape, jnp.float32)
        for a in range(taps):
            total = jnp.where(tap == a, kernel[a : a + 1, :], total)
        return total

    def build(s, carry):
        meta = meta_in[s]
        kernel_u = jnp.zeros((taps, slots), jnp.float32)
        kernel_v = jnp.zeros((taps, slots), jnp.float32)
        for o in range(levels):
            column = jnp.broadcast_to(taper[:, o : o + 1], (taps, slots))
            kernel_u = jnp.where(meta[2:3, :] == o, column, kernel_u)
            kernel_v = jnp.where(meta[3:4, :] == o, column, kernel_v)
        spread_u = spread(kernel_u, meta[0:1, :], cell)
        spread_v = spread(kernel_v, meta[1:2, :], cell)
        edge_v = spread(kernel_v, meta[1:2, :], edge)
        at = pl.ds(pl.multiple_of(s * slots, LANES), slots)
        for i in range(TS):
            w_main[i * TS : (i + 1) * TS, at] = (spread_u[i : i + 1, :] * spread_v).astype(
                jnp.bfloat16
            )
        for j in range(2 * RIM):
            w_rim[j * TS : (j + 1) * TS, at] = (spread_u * edge_v[j : j + 1, :]).astype(
                jnp.bfloat16
            )
        return carry

    lax.fori_loop(0, count, build, 0)

    for d in range(0, count, 2):
        if d:
            row_copy(d).wait_recv()
        row_copy(d + 1).wait_recv()
        pair = (me if d == 0 else peers[d]) // 2
        block = rows_in[pl.ds(2 * pair, 2)].reshape(2 * slots, width)
        at = pl.ds(pl.multiple_of(pair * 2 * slots, 2 * LANES), 2 * slots)
        term = jnp.dot(w_rim[:, at], block, preferred_element_type=jnp.float32)
        if d == 0:
            rim_sum[...] = term
        elif d < count - 2:
            rim_sum[...] += term
        else:
            whole = (rim_sum[...] + term).astype(jnp.bfloat16)
            rim_out[0] = whole[: RIM * TS]
            rim_out[1] = whole[RIM * TS :]

    has_low = me > 0
    has_high = me < count - 1

    def rim_copy(side):
        return pltpu.make_async_remote_copy(
            src_ref=rim_out.at[side], dst_ref=rim_in.at[1 - side],
            send_sem=rim_send.at[side], recv_sem=rim_recv.at[1 - side],
            device_id={"tile": me - 1 + 2 * side}, device_id_type=MESH,
        )

    def rim_arrival(side):
        return pltpu.make_async_remote_copy(
            src_ref=rim_out.at[side], dst_ref=rim_in.at[side],
            send_sem=rim_send.at[side], recv_sem=rim_recv.at[side],
            device_id={"tile": me - 1 + 2 * side}, device_id_type=MESH,
        )

    for side, present in ((0, has_low), (1, has_high)):
        @pl.when(present)
        def _(side=side):
            rim_copy(side).start()

    everything = rows_in[...].reshape(count * slots, width)
    part = TS * TS // 4
    for m in range(4):
        total = jnp.dot(
            w_main[m * part : (m + 1) * part, :], everything, preferred_element_type=jnp.float32
        )
        out[m * part // TS : (m + 1) * part // TS] = total.reshape(part // TS, TS, width)

    place = lax.broadcasted_iota(jnp.int32, (8 * TS, RIM * TS), 0)
    origin = lax.broadcasted_iota(jnp.int32, (8 * TS, RIM * TS), 1)
    for side, present in ((0, has_low), (1, has_high)):
        @pl.when(present)
        def _(side=side):
            rim_arrival(side).wait_recv()
            wanted = (origin % TS) * 8 + origin // TS + RIM * side
            put = jnp.where(place == wanted, 1.0, 0.0).astype(jnp.bfloat16)
            extra = jnp.dot(put, rim_in[side], preferred_element_type=jnp.float32)
            first = (TS - 8) * side
            out[:, first : first + 8, :] += extra.reshape(TS, 8, width)
            rim_copy(side).wait_send()

    for d in far_first:
        meta_copy(d).wait_send()
        row_copy(d).wait_send()


def line_body(visibilities, send_list, pixels, offsets, taper):
    count, slots = send_list.shape
    width = visibilities.shape[1]
    cells = TS * TS
    rim_cells = 2 * RIM * TS
    dma = pltpu.SemaphoreType.DMA
    vmem = pl.BlockSpec(memory_space=pltpu.VMEM)
    result = pl.pallas_call(
        line_kernel,
        out_shape=pltpu.VMEM((TS, TS, width), jnp.float32),
        in_specs=[pl.BlockSpec(memory_space=pltpu.HBM)] * 5,
        out_specs=vmem,
        scratch_shapes=[
            pltpu.VMEM(visibilities.shape, visibilities.dtype),
            pltpu.VMEM(send_list.shape, send_list.dtype),
            pltpu.VMEM(pixels.shape, pixels.dtype),
            pltpu.VMEM(offsets.shape, offsets.dtype),
            pltpu.VMEM(taper.shape, taper.dtype),
            dma((5,)),
            pltpu.VMEM((count, slots, width), jnp.bfloat16),
            pltpu.VMEM((count, slots, width), jnp.bfloat16),
            pltpu.VMEM((count, 8, slots), jnp.int32),
            pltpu.VMEM((count, 8, slots), jnp.int32),
            pltpu.VMEM((cells, count * slots), jnp.bfloat16),
            pltpu.VMEM((rim_cells, count * slots), jnp.bfloat16),
            pltpu.VMEM((rim_cells, width), jnp.float32),
            pltpu.VMEM((2, rim_cells // 2, width), jnp.bfloat16),
            pltpu.VMEM((2, rim_cells // 2, width), jnp.bfloat16),
            dma((count,)), dma((count,)), dma((count,)), dma((count,)), dma((2,)), dma((2,)),
        ],
        compiler_params=pltpu.CompilerParams(
            collective_id=0, has_side_effects=True, vmem_limit_bytes=48 * 1024 * 1024
        ),
    )(*(
        pltpu.with_memory_space_constraint(x, pltpu.HBM)
        for x in (visibilities, send_list, pixels, offsets, taper)
    ))
    return result[None]


def passed_along(value, axis, by):
    count = lax.axis_size(axis)
    pairs = [(i, i + by) for i in range(count) if 0 <= i + by < count]
    return lax.ppermute(value, axis, pairs)


def spread(kernel, pixel, padded_side):
    cell_index = jnp.arange(padded_side, dtype=jnp.int32)[:, None] - pixel[None, :]
    tap_index = jnp.arange(kernel.shape[0], dtype=jnp.int32)[:, None, None]
    return jnp.sum(jnp.where(cell_index[None] == tap_index, kernel[:, None, :], 0.0), axis=0)


def place_block(block_rows, block_meta, taper, padded_side):
    levels = jnp.arange(taper.shape[1], dtype=jnp.int32)[:, None]
    select_u = (levels == block_meta[2][None, :]).astype(jnp.float32)
    select_v = (levels == block_meta[3][None, :]).astype(jnp.float32)
    kernel_u = jnp.dot(
        taper, select_u, precision=lax.Precision.HIGHEST, preferred_element_type=jnp.float32
    )
    kernel_v = jnp.dot(
        taper, select_v, precision=lax.Precision.HIGHEST, preferred_element_type=jnp.float32
    )
    spread_u = spread(kernel_u, block_meta[0], padded_side)
    spread_v = spread(kernel_v, block_meta[1], padded_side)
    weights = (spread_u[:, None, :] * spread_v[None, :, :]).astype(jnp.bfloat16)
    weights = weights.reshape(padded_side * padded_side, -1)
    return jnp.dot(weights, block_rows, preferred_element_type=jnp.float32)


def grid_blocks(slot_rows, slot_meta, taper, padded_side, block_size, block_count):
    width = slot_rows.shape[1]

    def one_block(index, running):
        start = index * block_size
        block_rows = lax.dynamic_slice_in_dim(slot_rows, start, block_size, 0)
        block_meta = lax.dynamic_slice_in_dim(slot_meta, start, block_size, 1)
        return running + place_block(block_rows, block_meta, taper, padded_side)

    initial = jnp.zeros((padded_side * padded_side, width), jnp.float32)
    return lax.fori_loop(0, block_count, one_block, initial)


def body(visibilities, send_list, pixels, offsets, taper):
    tile_count = lax.axis_size("tile")
    tiles_x = tile_count // TILES_Y
    slot_cap = send_list.shape[1]
    components = visibilities.shape[1]
    padded_side = TS + 8
    slot_total = tile_count * slot_cap
    block_size = min(512, slot_total)
    is_live = send_list >= 0
    picked = jnp.where(is_live, send_list, 0).reshape(-1)
    gathered = jnp.take(visibilities, picked, axis=0).reshape(tile_count, slot_cap, components)
    outgoing = jnp.where(is_live[:, :, None], gathered, jnp.zeros_like(gathered))
    live_flag = is_live.reshape(1, -1)
    slot_meta = jnp.concatenate(
        [
            jnp.take(pixels, picked, axis=1),
            jnp.take(offsets, picked, axis=1),
            live_flag.astype(jnp.int32),
        ],
        0,
    )
    slot_meta = (
        jnp.where(live_flag, slot_meta, 0).reshape(5, tile_count, slot_cap).transpose(1, 0, 2)
    )
    arrived_meta = lax.all_to_all(slot_meta, "tile", split_axis=0, concat_axis=0, tiled=True)
    meta_rows = arrived_meta.transpose(1, 0, 2).reshape(5, slot_total)
    arrived = lax.all_to_all(outgoing, "tile", split_axis=0, concat_axis=0, tiled=True)
    padded_grid = grid_blocks(
        arrived.reshape(slot_total, components),
        meta_rows,
        taper,
        padded_side,
        block_size,
        slot_total // block_size,
    )
    padded_grid = padded_grid.reshape(padded_side, padded_side, components)
    tile_row = lax.axis_index("tile") % TILES_Y
    source_start = {-1: TS + 4, 0: 4, 1: 0}
    target_start = {-1: 0, 0: 0, 1: TS - 4}
    span = {-1: 4, 0: TS, 1: 4}
    result = padded_grid[4 : TS + 4, 4 : TS + 4]
    for step_x in (-1, 0, 1):
        for step_y in (-1, 0, 1):
            if step_x == 0 and step_y == 0 or (step_x != 0 and tiles_x == 1):
                continue
            piece = padded_grid[
                source_start[step_x] : source_start[step_x] + span[step_x],
                source_start[step_y] : source_start[step_y] + span[step_y],
            ]
            incoming = passed_along(piece, "tile", -(step_x * TILES_Y + step_y))
            inside = (tile_row + step_y >= 0) & (tile_row + step_y < TILES_Y)
            incoming = jnp.where(inside, incoming, 0.0)
            result = result.at[
                target_start[step_x] : target_start[step_x] + span[step_x],
                target_start[step_y] : target_start[step_y] + span[step_y],
            ].add(incoming)
    return result[None]


def solution(mesh):
    placed = (
        P("tile", "chan"),
        P(("chan", "tile"), None),
        P(None, ("chan", "tile")),
        P(None, ("chan", "tile")),
        P(),
    )
    one_line = mesh.shape["tile"] == TILES_Y

    def chosen(visibilities, send_list, *rest):
        fits = one_line and send_list.shape[1] == LANES and visibilities.shape[0] % LANES == 0
        return (line_body if fits else body)(visibilities, send_list, *rest)

    return jax.shard_map(
        chosen, mesh=mesh, in_specs=placed, out_specs=P("tile", None, None, "chan"), check_vma=False
    )
```

```python
import jax
import jax.numpy as jnp
from jax import lax
from jax.experimental import pallas as pl
from jax.experimental.pallas import tpu as pltpu
from jax.sharding import PartitionSpec as P

TS = 32
TILES_Y = 8
RIM = 4
LANES = 128
MESH = pl.DeviceIdType.MESH


def flip(index, distance):
    total = 0
    for bit in (1, 2, 4):
        own = (index // bit) % 2
        total = total + bit * (1 - own if distance & bit else own)
    return total


def line_kernel(
    vis_far, lists_far, pix_far, off_far, taper_far, out,
    vis, lists, pix, off, taper, load_sem, rows_out, rows_in, meta_out, meta_in, w_main, w_rim, rim_sum, rim_out, rim_in,
    row_send, row_recv, meta_send, meta_recv, rim_send, rim_recv,
):
    count, slots = lists.shape
    rows, width = vis.shape
    taps, levels = taper.shape
    me = lax.axis_index("tile")
    far_first = [d for d in range(count - 1, 1, -1)] + [1]
    peers = {d: flip(me, d) for d in range(1, count)}

    barrier = pltpu.get_barrier_semaphore()
    for d in far_first:
        pl.semaphore_signal(barrier, inc=1, device_id={"tile": peers[d]}, device_id_type=MESH)
    loads = [
        pltpu.make_async_copy(far, near, load_sem.at[i])
        for i, (far, near) in enumerate(
            ((lists_far, lists), (pix_far, pix), (off_far, off), (taper_far, taper), (vis_far, vis))
        )
    ]
    for load in loads:
        load.start()

    for load in loads[:4]:
        load.wait()
    listed = lists[...]
    live = listed >= 0
    spot = jnp.where(live, listed, 0)
    packed = pix[0:1, :] + 32 * pix[1:2, :] + 1024 * off[0:1, :] + 16384 * off[1:2, :]
    inner = spot & (LANES - 1)
    outer = spot >> 7
    found = jnp.zeros((count, slots), jnp.int32)
    for b in range(rows // LANES):
        source = jnp.broadcast_to(packed[:, b * LANES : (b + 1) * LANES], (count, LANES))
        here = jnp.take_along_axis(source, inner, axis=1, mode="promise_in_bounds")
        found = jnp.where(outer == b, here, found)
    fields = (
        jnp.where(live, found & 31, -64),
        jnp.where(live, (found >> 5) & 31, -64),
        (found >> 10) & 15,
        (found >> 14) & 15,
    )
    for t in range(count):
        for f, field in enumerate(fields):
            meta_out[t, f : f + 1, :] = field[t : t + 1, :]

    def meta_copy(d):
        return pltpu.make_async_remote_copy(
            src_ref=meta_out.at[peers[d], 0:4], dst_ref=meta_in.at[me, 0:4],
            send_sem=meta_send.at[d], recv_sem=meta_recv.at[d],
            device_id={"tile": peers[d]}, device_id_type=MESH,
        )

    def row_copy(d):
        return pltpu.make_async_remote_copy(
            src_ref=rows_out.at[d], dst_ref=rows_in.at[me],
            send_sem=row_send.at[d], recv_sem=row_recv.at[d],
            device_id={"tile": peers[d]}, device_id_type=MESH,
        )

    lane = lax.broadcasted_iota(jnp.int32, (slots, LANES), 1)

    def pick(t):
        row = lists[pl.ds(t, 1), :]
        spread_list = jnp.broadcast_to(row, (LANES, slots)).T
        hot = [
            jnp.where(spread_list == lane + b * LANES, 1.0, 0.0).astype(jnp.bfloat16)
            for b in range(rows // LANES)
        ]
        return jnp.concatenate(hot, axis=1)

    loads[4].wait()
    for d in (6, 4):
        near = me if d == 0 else peers[d]
        hot = jnp.concatenate([pick(near), pick(peers[d + 1])], axis=0)
        got = jnp.dot(hot, vis[...], preferred_element_type=jnp.float32).astype(jnp.bfloat16)
        rows_out[d + 1] = got[slots:]
        if d == 0:
            rows_in[me] = got[:slots]
        else:
            rows_out[d] = got[:slots]
    pl.semaphore_wait(barrier, count - 1)
    for e in far_first:
        meta_copy(e).start()
    meta_in[me] = meta_out[me]
    for d in (6, 4, 7, 5):
        row_copy(d).start()
    for d in (2, 0):
        near = me if d == 0 else peers[d]
        hot = jnp.concatenate([pick(near), pick(peers[d + 1])], axis=0)
        got = jnp.dot(hot, vis[...], preferred_element_type=jnp.float32).astype(jnp.bfloat16)
        rows_out[d + 1] = got[slots:]
        if d == 0:
            rows_in[me] = got[:slots]
        else:
            rows_out[d] = got[:slots]
    for d in (2, 3, 1):
        row_copy(d).start()

    for d in far_first:
        meta_copy(d).wait_recv()

    cell = lax.broadcasted_iota(jnp.int32, (TS, slots), 0) + RIM
    edge = lax.broadcasted_iota(jnp.int32, (2 * RIM, slots), 0)
    edge = jnp.where(edge >= RIM, edge + TS, edge)

    def spread(kernel, pixel, cells):
        tap = cells - pixel
        total = jnp.zeros(cells.shape, jnp.float32)
        for a in range(taps):
            total = jnp.where(tap == a, kernel[a : a + 1, :], total)
        return total

    def build(s, carry):
        meta = meta_in[s]
        kernel_u = jnp.zeros((taps, slots), jnp.float32)
        kernel_v = jnp.zeros((taps, slots), jnp.float32)
        for o in range(levels):
            column = jnp.broadcast_to(taper[:, o : o + 1], (taps, slots))
            kernel_u = jnp.where(meta[2:3, :] == o, column, kernel_u)
            kernel_v = jnp.where(meta[3:4, :] == o, column, kernel_v)
        spread_u = spread(kernel_u, meta[0:1, :], cell)
        spread_v = spread(kernel_v, meta[1:2, :], cell)
        edge_v = spread(kernel_v, meta[1:2, :], edge)
        at = pl.ds(pl.multiple_of(s * slots, LANES), slots)
        for i in range(TS):
            w_main[i * TS : (i + 1) * TS, at] = (spread_u[i : i + 1, :] * spread_v).astype(
                jnp.bfloat16
            )
        for j in range(2 * RIM):
            w_rim[j * TS : (j + 1) * TS, at] = (spread_u * edge_v[j : j + 1, :]).astype(
                jnp.bfloat16
            )
        return carry

    lax.fori_loop(0, count, build, 0)

    for d in range(0, count, 2):
        if d:
            row_copy(d).wait_recv()
        row_copy(d + 1).wait_recv()
        pair = (me if d == 0 else peers[d]) // 2
        block = rows_in[pl.ds(2 * pair, 2)].reshape(2 * slots, width)
        at = pl.ds(pl.multiple_of(pair * 2 * slots, 2 * LANES), 2 * slots)
        term = jnp.dot(w_rim[:, at], block, preferred_element_type=jnp.float32)
        if d == 0:
            rim_sum[...] = term
        elif d < count - 2:
            rim_sum[...] += term
        else:
            whole = (rim_sum[...] + term).astype(jnp.bfloat16)
            rim_out[0] = whole[: RIM * TS]
            rim_out[1] = whole[RIM * TS :]

    has_low = me > 0
    has_high = me < count - 1

    def rim_copy(side):
        return pltpu.make_async_remote_copy(
            src_ref=rim_out.at[side], dst_ref=rim_in.at[1 - side],
            send_sem=rim_send.at[side], recv_sem=rim_recv.at[1 - side],
            device_id={"tile": me - 1 + 2 * side}, device_id_type=MESH,
        )

    def rim_arrival(side):
        return pltpu.make_async_remote_copy(
            src_ref=rim_out.at[side], dst_ref=rim_in.at[side],
            send_sem=rim_send.at[side], recv_sem=rim_recv.at[side],
            device_id={"tile": me - 1 + 2 * side}, device_id_type=MESH,
        )

    for side, present in ((0, has_low), (1, has_high)):
        @pl.when(present)
        def _(side=side):
            rim_copy(side).start()

    everything = rows_in[...].reshape(count * slots, width)
    part = TS * TS // 4
    for m in range(4):
        total = jnp.dot(
            w_main[m * part : (m + 1) * part, :], everything, preferred_element_type=jnp.float32
        )
        out[m * part // TS : (m + 1) * part // TS] = total.reshape(part // TS, TS, width)

    place = lax.broadcasted_iota(jnp.int32, (8 * TS, RIM * TS), 0)
    origin = lax.broadcasted_iota(jnp.int32, (8 * TS, RIM * TS), 1)
    for side, present in ((0, has_low), (1, has_high)):
        @pl.when(present)
        def _(side=side):
            rim_arrival(side).wait_recv()
            wanted = (origin % TS) * 8 + origin // TS + RIM * side
            put = jnp.where(place == wanted, 1.0, 0.0).astype(jnp.bfloat16)
            extra = jnp.dot(put, rim_in[side], preferred_element_type=jnp.float32)
            first = (TS - 8) * side
            out[:, first : first + 8, :] += extra.reshape(TS, 8, width)
            rim_copy(side).wait_send()

    for d in far_first:
        meta_copy(d).wait_send()
        row_copy(d).wait_send()


def line_body(visibilities, send_list, pixels, offsets, taper):
    count, slots = send_list.shape
    width = visibilities.shape[1]
    cells = TS * TS
    rim_cells = 2 * RIM * TS
    dma = pltpu.SemaphoreType.DMA
    vmem = pl.BlockSpec(memory_space=pltpu.VMEM)
    result = pl.pallas_call(
        line_kernel,
        out_shape=pltpu.VMEM((TS, TS, width), jnp.float32),
        in_specs=[pl.BlockSpec(memory_space=pltpu.HBM)] * 5,
        out_specs=vmem,
        scratch_shapes=[
            pltpu.VMEM(visibilities.shape, visibilities.dtype),
            pltpu.VMEM(send_list.shape, send_list.dtype),
            pltpu.VMEM(pixels.shape, pixels.dtype),
            pltpu.VMEM(offsets.shape, offsets.dtype),
            pltpu.VMEM(taper.shape, taper.dtype),
            dma((5,)),
            pltpu.VMEM((count, slots, width), jnp.bfloat16),
            pltpu.VMEM((count, slots, width), jnp.bfloat16),
            pltpu.VMEM((count, 8, slots), jnp.int32),
            pltpu.VMEM((count, 8, slots), jnp.int32),
            pltpu.VMEM((cells, count * slots), jnp.bfloat16),
            pltpu.VMEM((rim_cells, count * slots), jnp.bfloat16),
            pltpu.VMEM((rim_cells, width), jnp.float32),
            pltpu.VMEM((2, rim_cells // 2, width), jnp.bfloat16),
            pltpu.VMEM((2, rim_cells // 2, width), jnp.bfloat16),
            dma((count,)), dma((count,)), dma((count,)), dma((count,)), dma((2,)), dma((2,)),
        ],
        compiler_params=pltpu.CompilerParams(
            collective_id=0, has_side_effects=True, vmem_limit_bytes=48 * 1024 * 1024
        ),
    )(*(
        pltpu.with_memory_space_constraint(x, pltpu.HBM)
        for x in (visibilities, send_list, pixels, offsets, taper)
    ))
    return result[None]


def passed_along(value, axis, by):
    count = lax.axis_size(axis)
    pairs = [(i, i + by) for i in range(count) if 0 <= i + by < count]
    return lax.ppermute(value, axis, pairs)


def spread(kernel, pixel, padded_side):
    cell_index = jnp.arange(padded_side, dtype=jnp.int32)[:, None] - pixel[None, :]
    tap_index = jnp.arange(kernel.shape[0], dtype=jnp.int32)[:, None, None]
    return jnp.sum(jnp.where(cell_index[None] == tap_index, kernel[:, None, :], 0.0), axis=0)


def place_block(block_rows, block_meta, taper, padded_side):
    levels = jnp.arange(taper.shape[1], dtype=jnp.int32)[:, None]
    select_u = (levels == block_meta[2][None, :]).astype(jnp.float32)
    select_v = (levels == block_meta[3][None, :]).astype(jnp.float32)
    kernel_u = jnp.dot(
        taper, select_u, precision=lax.Precision.HIGHEST, preferred_element_type=jnp.float32
    )
    kernel_v = jnp.dot(
        taper, select_v, precision=lax.Precision.HIGHEST, preferred_element_type=jnp.float32
    )
    spread_u = spread(kernel_u, block_meta[0], padded_side)
    spread_v = spread(kernel_v, block_meta[1], padded_side)
    weights = (spread_u[:, None, :] * spread_v[None, :, :]).astype(jnp.bfloat16)
    weights = weights.reshape(padded_side * padded_side, -1)
    return jnp.dot(weights, block_rows, preferred_element_type=jnp.float32)


def grid_blocks(slot_rows, slot_meta, taper, padded_side, block_size, block_count):
    width = slot_rows.shape[1]

    def one_block(index, running):
        start = index * block_size
        block_rows = lax.dynamic_slice_in_dim(slot_rows, start, block_size, 0)
        block_meta = lax.dynamic_slice_in_dim(slot_meta, start, block_size, 1)
        return running + place_block(block_rows, block_meta, taper, padded_side)

    initial = jnp.zeros((padded_side * padded_side, width), jnp.float32)
    return lax.fori_loop(0, block_count, one_block, initial)


def body(visibilities, send_list, pixels, offsets, taper):
    tile_count = lax.axis_size("tile")
    tiles_x = tile_count // TILES_Y
    slot_cap = send_list.shape[1]
    components = visibilities.shape[1]
    padded_side = TS + 8
    slot_total = tile_count * slot_cap
    block_size = min(512, slot_total)
    is_live = send_list >= 0
    picked = jnp.where(is_live, send_list, 0).reshape(-1)
    gathered = jnp.take(visibilities, picked, axis=0).reshape(tile_count, slot_cap, components)
    outgoing = jnp.where(is_live[:, :, None], gathered, jnp.zeros_like(gathered))
    live_flag = is_live.reshape(1, -1)
    slot_meta = jnp.concatenate(
        [
            jnp.take(pixels, picked, axis=1),
            jnp.take(offsets, picked, axis=1),
            live_flag.astype(jnp.int32),
        ],
        0,
    )
    slot_meta = (
        jnp.where(live_flag, slot_meta, 0).reshape(5, tile_count, slot_cap).transpose(1, 0, 2)
    )
    arrived_meta = lax.all_to_all(slot_meta, "tile", split_axis=0, concat_axis=0, tiled=True)
    meta_rows = arrived_meta.transpose(1, 0, 2).reshape(5, slot_total)
    arrived = lax.all_to_all(outgoing, "tile", split_axis=0, concat_axis=0, tiled=True)
    padded_grid = grid_blocks(
        arrived.reshape(slot_total, components),
        meta_rows,
        taper,
        padded_side,
        block_size,
        slot_total // block_size,
    )
    padded_grid = padded_grid.reshape(padded_side, padded_side, components)
    tile_row = lax.axis_index("tile") % TILES_Y
    source_start = {-1: TS + 4, 0: 4, 1: 0}
    target_start = {-1: 0, 0: 0, 1: TS - 4}
    span = {-1: 4, 0: TS, 1: 4}
    result = padded_grid[4 : TS + 4, 4 : TS + 4]
    for step_x in (-1, 0, 1):
        for step_y in (-1, 0, 1):
            if step_x == 0 and step_y == 0 or (step_x != 0 and tiles_x == 1):
                continue
            piece = padded_grid[
                source_start[step_x] : source_start[step_x] + span[step_x],
                source_start[step_y] : source_start[step_y] + span[step_y],
            ]
            incoming = passed_along(piece, "tile", -(step_x * TILES_Y + step_y))
            inside = (tile_row + step_y >= 0) & (tile_row + step_y < TILES_Y)
            incoming = jnp.where(inside, incoming, 0.0)
            result = result.at[
                target_start[step_x] : target_start[step_x] + span[step_x],
                target_start[step_y] : target_start[step_y] + span[step_y],
            ].add(incoming)
    return result[None]


def solution(mesh):
    placed = (
        P("tile", "chan"),
        P(("chan", "tile"), None),
        P(None, ("chan", "tile")),
        P(None, ("chan", "tile")),
        P(),
    )
    one_line = mesh.shape["tile"] == TILES_Y

    def chosen(visibilities, send_list, *rest):
        fits = one_line and send_list.shape[1] == LANES and visibilities.shape[0] % LANES == 0
        return (line_body if fits else body)(visibilities, send_list, *rest)

    return jax.shard_map(
        chosen, mesh=mesh, in_specs=placed, out_specs=P("tile", None, None, "chan"), check_vma=False
    )
```
